256 devices in a mesh: dp: 4 (over x), seq: 64 (over z, y, core).
Axes of the slice: x: 4, y: 4, z: 8, core: 2. Of those that a mesh axis runs over, the one named last changes fastest.
Arguments:
- latents: bfloat16 [4, 64, 256, 1152], P('dp', 'seq'), may hold values from -16 to 16
- in_weight: bfloat16 [1152, 3456], replicated
- out_weight: bfloat16 [1152, 1152], replicated, may hold values from -0.1875 to 0.1875
- cotangent: bfloat16 [4, 64, 256, 1152], P('dp', 'seq'), may hold values from -6 to 6
- clip_lengths: int32 [4, 4], P('dp'), may hold values from 1 to 32, 64 in all within a row
Outputs:
- mixed: bfloat16 [4, 64, 256, 1152], P('dp', 'seq')
- grad_latents: bfloat16 [4, 64, 256, 1152], P('dp', 'seq')
- out_grad: float32 [1152, 1152], P('seq')
The draws below stay inside these ranges and needn't reach their ends.
Inputs may be any that keep to these rules, and one draw needn't show every extreme that they name: `clip_lengths`: the 4 lengths of a sequence sum to 64; in every sequence the longest is exactly 32.
All inputs are finite; a program needn't handle non-finite values.
Results may differ from the reference program's by a relative error of at most 0.013.
The reference program's roundings to bfloat16 on the way count: a program that leaves them out, or rounds other values in their place, can miss the bound.
Values may be sent and summed in bfloat16 or wider, within the bound.
A program may use at most 128 MiB of HBM per device.

```python
import math
import jax
import jax.numpy as jnp
import numpy as np
from jax import lax

D = 1152
HEADS = 16
HD = 72
P_SIZE = 256
CLIPS = 4
FRAMES = 64
MAXCLIP = 32
N_DP = 4


def draw_in_weight(key, part):
    key = jax.random.fold_in(key, 7)
    inner = HEADS * HD
    base = jax.random.normal(key, (D, 3 * inner), jnp.float32) * D ** (-0.5)
    return base.astype(jnp.bfloat16)


def with_spikes(values, rng, source, target, shards_of, factor):
    def block_of(dim):
        return (jnp.arange(values.shape[dim]) // (values.shape[dim] // shards_of)).reshape((-1,) + (1,) * (values.ndim - 1 - dim))

    near = jax.random.permutation(rng, shards_of)[block_of(target)]
    far = (block_of(target) + shards_of // 2) % shards_of
    return jnp.where((block_of(source) == near) | (block_of(source) == far), factor * values, values)


def shard_levels(stream_key, extent, pieces, least, high):
    def one(dim, blocks):
        draws = jax.random.uniform(jax.random.fold_in(jax.random.fold_in(stream_key, 6), dim), (blocks,), jnp.float32, least / len(pieces), high / len(pieces))
        return jnp.repeat(jnp.exp(draws), extent[dim] // blocks).reshape((-1,) + (1,) * (len(extent) - dim - 1))

    loudness = one(*pieces[0])
    for cut in pieces[1:]:
        loudness = loudness * one(*cut)
    return loudness


def length_profile(amount, total, bound, lean):
    weights = [(1 << 20) // math.isqrt(standing ** lean) + 1 for standing in range(2, amount + 1)]
    spare, counts = total - bound - (amount - 1), [1] * (amount - 1)
    while spare > 0:
        free = [i for i in range(amount - 1) if counts[i] < bound]
        whole, left = sum([weights[i] for i in free]), spare
        for i in free:
            extra = min(bound - counts[i], max(1, left * weights[i] // whole), spare)
            counts[i] = counts[i] + extra
            spare = spare - extra
    return np.array([bound] + counts)


def ragged_sizes(own_key, count, total, bound, skew):
    if count == 2:
        one = jax.random.randint(own_key, (), max(1, total - bound), min(bound, total - 1) + 1)
        return jnp.stack([one, total - one])
    sizes = jnp.asarray(length_profile(count, total, bound, skew), jnp.int32)
    pairs = (count - 1) // 2
    source_of, sink = sizes[1:1 + 2 * pairs:2], sizes[2:2 + 2 * pairs:2]
    margin = jnp.minimum(source_of - 1, bound - sink)
    passed = jax.random.randint(jax.random.fold_in(own_key, 1), (pairs,), 0, 1 << 20) % (margin + 1)
    sizes = sizes.at[1:1 + 2 * pairs:2].set(source_of - passed).at[2:2 + 2 * pairs:2].set(sink + passed)
    return sizes[jax.random.permutation(jax.random.fold_in(own_key, 2), count)]


def bell_draw(stream_key, extent, scale, limit, shards=(), held_as=jnp.bfloat16):
    result = scale * jax.random.normal(stream_key, extent, jnp.float32)
    if shards:
        result = result * shard_levels(stream_key, extent, shards, -0.22, 0.18)
    return jnp.clip(result, -limit, limit).astype(held_as)


def gaussian_with(own_key, dims, scale, most, cuts, heavy, kind=jnp.bfloat16):
    values = scale * jax.random.normal(own_key, dims, jnp.float32)
    if cuts:
        values = values * shard_levels(own_key, dims, cuts, -0.22, 0.18)
    return jnp.clip(with_spikes(values, jax.random.fold_in(own_key, 3), *heavy), -most, most).astype(kind)


def setup_inputs(seed: int = 0) -> dict:
    key_of = jax.random.split(jax.random.key(seed), 6)
    return {
        "latents": gaussian_with(key_of[0], (N_DP, FRAMES, P_SIZE, D), 1.0, 16.0, ((0, 4), (1, 64)), (1, 3, 64, 4.0)),
        "in_weight": draw_in_weight(jax.random.fold_in(key_of[5], 71), 0),
        "out_weight": bell_draw(key_of[2], (HEADS * HD, D), (HEADS * HD) ** -0.5, 0.1875),
        "cotangent": bell_draw(key_of[3], (N_DP, FRAMES, P_SIZE, D), 1.0, 6.0, ((0, 4), (1, 64))),
        "clip_lengths": jax.vmap(lambda own: ragged_sizes(own, CLIPS, FRAMES, MAXCLIP, 1))(jax.random.split(key_of[4], N_DP)).reshape((N_DP, CLIPS)).astype(jnp.int32),
    }


def clip_index(lengths, frames):
    ends = jnp.cumsum(lengths).astype(jnp.int32)
    position = jnp.arange(frames, dtype=jnp.int32)
    return lax.optimization_barrier(jnp.sum((ends[None, :] <= position[:, None]).astype(jnp.int32), axis=1))

def one_sequence(latent_seq, cot_seq, lengths, in_weight, out_weight):
    frames, patches, width = latent_seq.shape
    inner = HEADS * HD
    tok_rows = latent_seq.reshape(frames * patches, width)
    projected = jnp.dot(tok_rows, in_weight, preferred_element_type=jnp.float32).astype(jnp.bfloat16)
    split = projected.reshape(frames, patches, 3, HEADS, HD).astype(jnp.float32)
    query, key_rows, value_rows = (split[:, :, 0], split[:, :, 1], split[:, :, 2])
    clip = clip_index(lengths, frames)
    same = clip[:, None] == clip[None, :]
    scale = 1.0 / jnp.sqrt(jnp.float32(HD))
    scores = jnp.einsum('fphd,gphd->phfg', query, key_rows) * scale
    scores = jnp.where(same[None, None], scores, -jnp.inf)
    weights32 = jax.nn.softmax(scores, axis=-1)
    weights = weights32.astype(jnp.bfloat16).astype(jnp.float32)
    attended = jnp.einsum('phfg,gphd->fphd', weights, value_rows).astype(jnp.bfloat16)
    att_rows = attended.reshape(frames * patches, inner)
    mixed = jnp.dot(att_rows, out_weight, preferred_element_type=jnp.float32).astype(jnp.bfloat16)
    cot_rows = cot_seq.reshape(frames * patches, width)
    grad_att = jnp.dot(cot_rows, out_weight.T, preferred_element_type=jnp.float32).astype(jnp.bfloat16)
    out_grad = jnp.dot(att_rows.T, cot_rows, preferred_element_type=jnp.float32)
    grad_heads = grad_att.reshape(frames, patches, HEADS, HD).astype(jnp.float32)
    grad_weights = jnp.einsum('fphd,gphd->phfg', grad_heads, value_rows)
    grad_values = jnp.einsum('phfg,fphd->gphd', weights, grad_heads).astype(jnp.bfloat16)
    totals = lax.optimization_barrier(jnp.sum(weights32 * grad_weights, axis=-1, keepdims=True))
    grad_scores = (weights32 * (grad_weights - totals) * scale).astype(jnp.bfloat16).astype(jnp.float32)
    grad_query = jnp.einsum('phfg,gphd->fphd', grad_scores, key_rows).astype(jnp.bfloat16)
    grad_keys = jnp.einsum('phfg,fphd->gphd', grad_scores, query).astype(jnp.bfloat16)
    grad_proj = jnp.stack([grad_query, grad_keys, grad_values], axis=2).reshape(frames * patches, 3 * inner)
    grad_lat = jnp.dot(grad_proj, in_weight.T, preferred_element_type=jnp.float32).astype(jnp.bfloat16)
    return (mixed.reshape(frames, patches, width), grad_lat.reshape(frames, patches, width), out_grad)

def reference(latents, in_weight, out_weight, cotangent, clip_lengths):

    def step(items):
        return one_sequence(items[0], items[1], items[2], in_weight, out_weight)
    mixed, grad_latents, out_grads = lax.map(step, (latents, cotangent, clip_lengths))
    return (mixed, grad_latents, lax.optimization_barrier(jnp.sum(out_grads, axis=0)))
```

```python
import functools

import jax
import jax.numpy as jnp
from jax import lax
from jax.experimental import pallas as pl
from jax.experimental.pallas import tpu as pltpu
from jax.sharding import PartitionSpec as P

MESH = pl.DeviceIdType.MESH
BF16 = jnp.bfloat16
F32 = jnp.float32
HEADS, HD = 16, 72
INNER = HEADS * HD
ZS, YS, CS, XS = 8, 4, 2, 4
SEQ = ZS * YS * CS
SCALE = float(HD) ** -0.5
NT = (((1,), (1,)), ((), ()))
NN = (((1,), (0,)), ((), ()))
TN = (((0,), (0,)), ((), ()))


def dot(a, b, dims=NN):
    return lax.dot_general(a, b, dims, preferred_element_type=F32)


def window(h):
    lo = h * HD // 128 * 128
    hi = -(-(h * HD + HD) // 128) * 128
    return lo, hi


def lane_mask(h, lo, hi, dtype):
    lane = lax.broadcasted_iota(jnp.int32, (1, hi - lo), 1) + lo
    return ((lane >= h * HD) & (lane < h * HD + HD)).astype(dtype)


class Columns:
    def __init__(self, ref, rows, base):
        self.ref, self.rows, self.base, self.cur = ref, rows, base, None

    def add(self, h, out, lo, hi):
        for t in range(lo, hi, 128):
            part = out[:, t - lo : t - lo + 128]
            if t >= h * HD:
                self.cur = part
            else:
                lane = lax.broadcasted_iota(jnp.int32, (1, 128), 1) + t
                self.cur = jnp.where(lane >= h * HD, part, self.cur)
            if t + 128 <= h * HD + HD:
                self.ref[self.rows, self.base + t : self.base + t + 128] = self.cur.astype(BF16)


def kernel(
    lat_ref, cot_ref, len_ref, inw_hbm, outw_hbm,
    mixed_o, glat_o, og_o,
    xs, xr, cs, cr, ms, gs, inw, outw, qkv, w32s, att, cp, ga, gp, attT, paT, pc,
    gsend, gxr, gown, ysend, yr, zsend, zr, ogs, ogr, amask,
    wsem, lsem, ssem, rsem, psem_s, psem_r, xsem_s, xsem_r, ysem_s, ysem_r, zsem_s, zsem_r, bsem_s, bsem_r,
):
    x = lax.axis_index("dp")
    me = lax.axis_index("seq")
    z, y, c = me // (YS * CS), me // CS % YS, me % CS

    w_in = pltpu.make_async_copy(inw_hbm, inw, wsem.at[0])
    w_out = pltpu.make_async_copy(outw_hbm, outw, wsem.at[1])
    w_in.start()
    w_out.start()

    def peer(j):
        i, r = j // 8, 7 - j % 8
        dz = 4 + i // 2 - i % 2 * i
        return (z + dz) % ZS * (YS * CS) + (y + r // CS) % YS * CS + (c + r) % CS

    barrier = pltpu.get_barrier_semaphore()

    @pl.loop(0, SEQ - 1)
    def _(j):
        pl.semaphore_signal(barrier, inc=1, device_id=(x, peer(j)), device_id_type=MESH)

    for dx in range(1, XS):
        for dc in range(CS):
            pl.semaphore_signal(
                barrier, inc=1, device_id=((x + dx) % XS, z * 8 + y * 2 + (c + dc) % CS), device_id_type=MESH
            )

    xs[...] = lat_ref[...].reshape(SEQ, 4, INNER)
    pl.semaphore_wait(barrier, SEQ - 1 + (XS - 1) * CS)

    def exchange(k, src, dst):
        @pl.loop(0, SEQ - 1)
        def _(j):
            d = peer(j)
            pltpu.make_async_remote_copy(
                src_ref=src.at[d], dst_ref=dst.at[me], send_sem=ssem.at[k], recv_sem=rsem.at[k],
                device_id=(x, d), device_id_type=MESH,
            ).start()

        pltpu.make_async_copy(src.at[me], dst.at[me], lsem.at[k]).start()

    def arrived(k, src, dst):
        pltpu.make_async_copy(src.at[me], dst.at[me], lsem.at[k]).wait()
        part = dst.at[pl.ds(0, SEQ - 1)]
        pltpu.make_async_copy(part, part, rsem.at[k]).wait()

    def sent(k, src):
        part = src.at[pl.ds(0, SEQ - 1)]
        pltpu.make_async_copy(part, part, ssem.at[k]).wait()

    exchange(0, xs, xr)
    cs[...] = cot_ref[...].reshape(SEQ, 4, INNER)
    exchange(1, cs, cr)

    r_i = lax.broadcasted_iota(jnp.int32, (256, 256), 0)
    c_i = lax.broadcasted_iota(jnp.int32, (256, 256), 1)
    to_patch = (c_i == r_i % SEQ * 4 + r_i // SEQ).astype(BF16)
    to_frame = (r_i == c_i % SEQ * 4 + c_i // SEQ).astype(BF16)

    ends = [len_ref[0, 0]]
    for i in range(1, 4):
        ends.append(ends[-1] + len_ref[0, i])
    rows2 = lax.broadcasted_iota(jnp.int32, (128, 128), 0)
    cols2 = lax.broadcasted_iota(jnp.int32, (128, 128), 1)

    def clip_of(frame):
        total = jnp.zeros_like(frame)
        for e in ends:
            total = total + (frame >= e).astype(jnp.int32)
        return total

    same = (rows2 // SEQ == cols2 // SEQ) & (clip_of(rows2 % SEQ) == clip_of(cols2 % SEQ))
    amask[...] = jnp.where(same, 0.0, -jnp.inf).astype(F32)

    arrived(0, xs, xr)
    xp = dot(to_patch, xr[...].reshape(256, INNER)).astype(BF16)
    w_in.wait()

    @pl.loop(0, 9)
    def _(n):
        cols = pl.ds(pl.multiple_of(n * 384, 128), 384)
        qkv[:, cols] = dot(xp, inw[:, cols]).astype(BF16)

    @pl.loop(0, 2)
    def _(i):
        rows = pl.ds(pl.multiple_of(i * 128, 128), 128)
        place = Columns(att, rows, 0)
        for h in range(HEADS):
            lo, hi = window(h)
            q = qkv[rows, lo:hi] * lane_mask(h, lo, hi, BF16)
            k = qkv[rows, INNER + lo : INNER + hi]
            v = qkv[rows, 2 * INNER + lo : 2 * INNER + hi]
            s = dot(q, k, NT) * SCALE + amask[...]
            e = jnp.exp(s - jnp.max(s, axis=-1, keepdims=True))
            w = e / jnp.sum(e, axis=-1, keepdims=True)
            w32s[i, h] = w
            place.add(h, dot(w.astype(BF16), v), lo, hi)

    w_out.wait()
    att_f = dot(to_frame, att[...]).astype(BF16)
    ms[...] = dot(att_f, outw[...]).astype(BF16).reshape(SEQ, 4, INNER)
    exchange(2, ms, mixed_o)

    arrived(1, cs, cr)
    cp[...] = dot(to_patch, cr[...].reshape(256, INNER)).astype(BF16)
    attT[...] = att[...].T

    mate = z * 8 + y * 2 + (c + 1) % CS
    mine = pl.ds(pl.multiple_of(c * 576, 16), 576)
    theirs = pl.ds(pl.multiple_of((1 - c) * 576, 16), 576)
    to_mate = [
        pltpu.make_async_remote_copy(
            src_ref=s, dst_ref=d, send_sem=psem_s.at[k], recv_sem=psem_r.at[k],
            device_id=(x, mate), device_id_type=MESH,
        )
        for k, (s, d) in enumerate(((attT.at[theirs], paT), (cp, pc)))
    ]
    for t in to_mate:
        t.start()

    ga[...] = dot(cp[...], outw[...], NT).astype(BF16)

    for t in to_mate:
        t.wait()

    def block(j):
        own = attT[pl.ds(pl.multiple_of(c * 576 + j * 144, 16), 144), :]
        other = paT[pl.ds(pl.multiple_of(j * 144, 16), 144), :]
        return dot(own, cp[...]) + dot(other, pc[...])

    def x_copy(k):
        return pltpu.make_async_remote_copy(
            src_ref=gsend.at[k], dst_ref=gxr.at[k], send_sem=xsem_s.at[k], recv_sem=xsem_r.at[k],
            device_id=((x + k + 1) % XS, me), device_id_type=MESH,
        )

    for k in range(XS - 1):
        gsend[k] = block((x + k + 1) % XS).astype(BF16)
        x_copy(k).start()
    gown[...] = block(x)

    def y_copy(k):
        d = (y + k + 1) % YS
        return pltpu.make_async_remote_copy(
            src_ref=ysend.at[d], dst_ref=yr.at[k], send_sem=ysem_s.at[k], recv_sem=ysem_r.at[k],
            device_id=(x, z * 8 + d * 2 + c), device_id_type=MESH,
        )

    root = 4 * c + x
    z_copy = pltpu.make_async_remote_copy(
        src_ref=zsend, dst_ref=zr.at[z], send_sem=zsem_s, recv_sem=zsem_r,
        device_id=(x, root * 8 + y * 2 + c), device_id_type=MESH,
    )

    def x_stage():
        total = gown[...]
        for k in range(XS - 1):
            x_copy(k).wait()
            total = total + gxr[k].astype(F32)
        gown[...] = total
        for d in range(YS):
            ysend[d] = total[36 * d : 36 * d + 36].astype(BF16)
        for k in range(YS - 1):
            y_copy(k).start()

    def y_stage():
        total = ysend[y].astype(F32)
        for k in range(YS - 1):
            y_copy(k).wait()
            total = total + yr[k].astype(F32)
        zsend[...] = total.astype(BF16)

        @pl.when(z != root)
        def _():
            z_copy.start()

    def b_copy(dx, dc, k):
        return pltpu.make_async_remote_copy(
            src_ref=ogs.at[(c + dc) % CS], dst_ref=ogr, send_sem=bsem_s.at[k], recv_sem=bsem_r,
            device_id=((x + dx) % XS, z * 8 + y * 2 + (c + dc) % CS), device_id_type=MESH,
        )

    others = [(dx, dc) for dx in range(XS) for dc in range(CS) if (dx, dc) != (0, 0)]

    def z_stage():
        @pl.when(z == root)
        def _():
            part = zr.at[pl.ds(0, ZS - 1)]
            pltpu.make_async_copy(part, part, zsem_r).wait()
            zr[z] = zsend[...]
            total = zr[0].astype(F32)
            for k in range(1, ZS):
                total = total + zr[k].astype(F32)
            ogs[0] = total[:18]
            ogs[1] = total[18:]
            for k, (dx, dc) in enumerate(others):
                b_copy(dx, dc, k).start()

        @pl.when(z != root)
        def _():
            z_copy.wait_send()

    def last_stage():
        @pl.when(z == root)
        def _():
            og_o[...] = ogs[c]
            for k, (dx, dc) in enumerate(others):
                b_copy(dx, dc, k).wait_send()

        @pl.when(z != root)
        def _():
            b_copy(1, 0, 0).wait_recv()
            og_o[...] = ogr[...]

    @pl.loop(0, 2)
    def _(i):
        rows = pl.ds(pl.multiple_of(i * 128, 128), 128)
        pq, pk, pv = (Columns(gp, rows, INNER * t) for t in range(3))
        for h in range(HEADS):
            lo, hi = window(h)
            q = qkv[rows, lo:hi]
            k = qkv[rows, INNER + lo : INNER + hi]
            v = qkv[rows, 2 * INNER + lo : 2 * INNER + hi]
            g = ga[rows, lo:hi]
            w = w32s[i, h]
            dw = dot(g * lane_mask(h, lo, hi, BF16), v, NT)
            ds = (w * (dw - jnp.sum(w * dw, axis=-1, keepdims=True)) * SCALE).astype(BF16)
            pv.add(h, dot(w.astype(BF16), g, TN), lo, hi)
            pq.add(h, dot(ds, k), lo, hi)
            pk.add(h, dot(ds, q, TN), lo, hi)

    x_stage()

    @pl.loop(0, 9)
    def _(n):
        cols = pl.ds(pl.multiple_of(n * 128, 128), 128)
        cp[:, cols] = dot(gp[...], inw[cols, :], NT).astype(BF16)

    gs[...] = dot(to_frame, cp[...]).astype(BF16).reshape(SEQ, 4, INNER)
    exchange(3, gs, glat_o)
    y_stage()
    z_stage()
    last_stage()

    sent(0, xs)
    sent(1, cs)
    sent(2, ms)
    sent(3, gs)
    arrived(2, ms, mixed_o)
    arrived(3, gs, glat_o)


def body(latents, in_weight, out_weight, cotangent, clip_lengths):
    width = latents.shape[3]
    vmem = pl.BlockSpec(memory_space=pltpu.VMEM)
    hbm = pl.BlockSpec(memory_space=pl.ANY)
    msg = (SEQ, 4, INNER)
    tok = (256, INNER)
    dma = pltpu.SemaphoreType.DMA
    mixed, grad_latents, out_grad = pl.pallas_call(
        kernel,
        out_shape=[
            jax.ShapeDtypeStruct(msg, BF16),
            jax.ShapeDtypeStruct(msg, BF16),
            jax.ShapeDtypeStruct((18, INNER), F32),
        ],
        in_specs=[vmem, vmem, pl.BlockSpec(memory_space=pltpu.SMEM), hbm, hbm],
        out_specs=[hbm, hbm, vmem],
        scratch_shapes=[pltpu.VMEM(msg, BF16)] * 6
        + [
            pltpu.VMEM((INNER, 3 * INNER), BF16),
            pltpu.VMEM((INNER, INNER), BF16),
            pltpu.VMEM((256, 3 * INNER), BF16),
            pltpu.VMEM((2, HEADS, 128, 128), F32),
            pltpu.VMEM(tok, BF16),
            pltpu.VMEM(tok, BF16),
            pltpu.VMEM(tok, BF16),
            pltpu.VMEM((256, 3 * INNER), BF16),
            pltpu.VMEM((INNER, 256), BF16),
            pltpu.VMEM((576, 256), BF16),
            pltpu.VMEM(tok, BF16),
            pltpu.VMEM((3, 144, INNER), BF16),
            pltpu.VMEM((3, 144, INNER), BF16),
            pltpu.VMEM((144, INNER), F32),
            pltpu.VMEM((4, 36, INNER), BF16),
            pltpu.VMEM((3, 36, INNER), BF16),
            pltpu.VMEM((36, INNER), BF16),
            pltpu.VMEM((ZS, 36, INNER), BF16),
            pltpu.VMEM((2, 18, INNER), F32),
            pltpu.VMEM((18, INNER), F32),
            pltpu.VMEM((128, 128), F32),
            dma((2,)), dma((4,)), dma((4,)), dma((4,)),
            dma((2,)), dma((2,)), dma((3,)), dma((3,)), dma((3,)), dma((3,)),
            dma, dma, dma((7,)), dma,
        ],
        compiler_params=pltpu.CompilerParams(
            collective_id=0, has_side_effects=True, vmem_limit_bytes=56 << 20
        ),
        name="sublayer",
    )(
        latents.reshape(256, width), cotangent.reshape(256, width), clip_lengths, in_weight, out_weight,
    )
    return mixed.reshape(latents.shape), grad_latents.reshape(latents.shape), out_grad


def solution(mesh):
    placed = (P("dp", "seq", None, None), P(), P(), P("dp", "seq", None, None), P("dp", None))
    return jax.shard_map(
        body,
        mesh=mesh,
        in_specs=placed,
        out_specs=(P("dp", "seq", None, None), P("dp", "seq", None, None), P("seq", None)),
        check_vma=False,
    )
```

```python
import jax
import jax.numpy as jnp
from jax import lax
from jax.experimental import pallas as pl
from jax.experimental.pallas import tpu as pltpu
from jax.sharding import PartitionSpec as P

MESH = pl.DeviceIdType.MESH
BF16 = jnp.bfloat16
F32 = jnp.float32
HEADS, HD = 16, 72
INNER = HEADS * HD
ZS, YS, CS, XS = 8, 4, 2, 4
SEQ = ZS * YS * CS
SCALE = float(HD) ** -0.5
LOG2E = 1.4426950408889634
LEFT = 640
RIGHT = INNER - LEFT
NT = (((1,), (1,)), ((), ()))
NN = (((1,), (0,)), ((), ()))
TN = (((0,), (0,)), ((), ()))
OTHERS = [(dx, dc) for dx in range(XS) for dc in range(CS) if (dx, dc) != (0, 0)]
GROUP = 4


def dot(a, b, dims=NN):
    return lax.dot_general(a, b, dims, preferred_element_type=F32)


def kernel(
    lat_hbm, cot_hbm, len_ref, inw_hbm, outw_hbm,
    mixed_o, glat_o, og_o,
    latv, cotv, xs, xr, cs, cr, ms, gs, inw, inwT, outw, qkvT, w32s, attT, cp, gaT, gpT, glatT, paT, pc,
    gsx, grx, gsy, gry, gox, goy, ys1, yr1, ys2, yr2, zs1, zr1, zs2, zr2, og1s, og2s, og1, og2, amask,
    wsem, lsem, ssem, rsem, psem_s, psem_r, gsem_s, gsem_r, hsem_s, hsem_r, zsem_s, zsem_r, bsem_s, bsem_r,
):
    x = lax.axis_index("dp")
    me = lax.axis_index("seq")
    z, y, c = me // (YS * CS), me // CS % YS, me % CS

    def seq(zz, yy, cc):
        return zz * (YS * CS) + yy * CS + cc

    loads = [
        pltpu.make_async_copy(s, d, wsem.at[k])
        for k, (s, d) in enumerate(((lat_hbm, latv), (cot_hbm, cotv), (inw_hbm, inw), (outw_hbm, outw)))
    ]
    for t in loads:
        t.start()

    def peer(j):
        i, r = j // 8, 7 - j % 8
        dz = 4 + i // 2 - i % 2 * i
        return seq((z + dz) % ZS, (y + r // CS) % YS, (c + r) % CS)

    barrier = pltpu.get_barrier_semaphore()

    @pl.loop(0, SEQ - 1, unroll=9)
    def _(j):
        pl.semaphore_signal(barrier, inc=1, device_id=(x, peer(j)), device_id_type=MESH)

    for dx, dc in OTHERS[1:]:
        pl.semaphore_signal(
            barrier, inc=1, device_id=((x + dx) % XS, seq(z, y, (c + dc) % CS)), device_id_type=MESH
        )

    loads[0].wait()
    xs[...] = latv[...].reshape(SEQ, 4, INNER)
    pl.semaphore_wait(barrier, SEQ - 1 + len(OTHERS) - 1)

    def exchange(k, src, dst):
        @pl.loop(0, SEQ - 1, unroll=9)
        def _(j):
            d = peer(j)
            pltpu.make_async_remote_copy(
                src_ref=src.at[d], dst_ref=dst.at[me], send_sem=ssem.at[k], recv_sem=rsem.at[k],
                device_id=(x, d), device_id_type=MESH,
            ).start()

        pltpu.make_async_copy(src.at[me], dst.at[me], lsem.at[k]).start()

    def arrived(k, src, dst):
        pltpu.make_async_copy(src.at[me], dst.at[me], lsem.at[k]).wait()
        part = dst.at[pl.ds(0, SEQ - 1)]
        pltpu.make_async_copy(part, part, rsem.at[k]).wait()

    def sent(k, src):
        part = src.at[pl.ds(0, SEQ - 1)]
        pltpu.make_async_copy(part, part, ssem.at[k]).wait()

    exchange(0, xs, xr)
    loads[1].wait()
    cs[...] = cotv[...].reshape(SEQ, 4, INNER)

    r_i = lax.broadcasted_iota(jnp.int32, (256, 256), 0)
    c_i = lax.broadcasted_iota(jnp.int32, (256, 256), 1)
    to_patch = (c_i == r_i % SEQ * 4 + r_i // SEQ).astype(BF16)
    to_frame = (r_i == c_i % SEQ * 4 + c_i // SEQ).astype(BF16)

    ends = [len_ref[0, 0]]
    for i in range(1, 4):
        ends.append(ends[-1] + len_ref[0, i])
    rows2 = lax.broadcasted_iota(jnp.int32, (128, 128), 0)
    cols2 = lax.broadcasted_iota(jnp.int32, (128, 128), 1)

    def clip_of(frame):
        total = jnp.zeros_like(frame)
        for e in ends:
            total = total + (frame >= e).astype(jnp.int32)
        return total

    same = (rows2 // SEQ == cols2 // SEQ) & (clip_of(rows2 % SEQ) == clip_of(cols2 % SEQ))
    amask[...] = jnp.where(same, 0.0, -jnp.inf).astype(F32)

    loads[2].wait()

    @pl.loop(0, 9)
    def _(n):
        cols = pl.ds(pl.multiple_of(n * 384, 128), 384)
        inwT[cols, :] = inw[:, cols].T

    exchange(1, cs, cr)
    loads[3].wait()

    arrived(0, xs, xr)
    xp = dot(to_patch, xr[...].reshape(256, INNER)).astype(BF16)

    @pl.loop(0, 6)
    def _(n):
        out = dot(inwT[pl.ds(pl.multiple_of(n * 576, 16), 576), :], xp, NT)
        for i in range(8):
            qkvT[n * 8 + i] = out[HD * i : HD * i + HD].astype(BF16)


    def lanes(i):
        return slice(128 * i, 128 * i + 128)

    @pl.loop(0, HEADS // GROUP)
    def _(n):
        for i in range(2):
            outs = []
            for t in range(GROUP):
                h = n * GROUP + t
                s = dot(qkvT[HEADS + h, :, lanes(i)], qkvT[h, :, lanes(i)], TN) + amask[...]
                e = jnp.exp2((s - jnp.max(s, axis=0, keepdims=True)) * (SCALE * LOG2E))
                w = e / jnp.sum(e, axis=0, keepdims=True)
                w32s[i, h] = w
                outs.append(dot(qkvT[2 * HEADS + h, :, lanes(i)], w.astype(BF16)))
            rows = pl.ds(pl.multiple_of(n * (GROUP * HD), 16), GROUP * HD)
            attT[rows, lanes(i)] = jnp.concatenate(outs, axis=0).astype(BF16)

    mate = seq(z, y, 1 - c)
    theirs = pl.ds(pl.multiple_of((1 - c) * 576, 16), 576)

    def to_mate(k, src, dst):
        return pltpu.make_async_remote_copy(
            src_ref=src, dst_ref=dst, send_sem=psem_s.at[k], recv_sem=psem_r.at[k],
            device_id=(x, mate), device_id_type=MESH,
        )

    att_copy = to_mate(0, attT.at[theirs], paT)
    cot_copy = to_mate(1, cp, pc)
    att_copy.start()
    att_f = dot(to_frame, attT[...], NT).astype(BF16)
    ms[...] = dot(att_f, outw[...]).astype(BF16).reshape(SEQ, 4, INNER)
    exchange(2, ms, mixed_o)

    arrived(1, cs, cr)
    cp[...] = dot(to_patch, cr[...].reshape(256, INNER)).astype(BF16)
    cot_copy.start()

    @pl.loop(0, 2)
    def _(n):
        out = dot(outw[pl.ds(pl.multiple_of(n * 576, 16), 576), :], cp[...], NT)
        for i in range(8):
            gaT[n * 8 + i] = out[HD * i : HD * i + HD].astype(BF16)

    att_copy.wait()
    cot_copy.wait()

    def block(j, cols):
        own = attT[pl.ds(pl.multiple_of(c * 576 + j * 144, 16), 144), :]
        other = paT[pl.ds(pl.multiple_of(j * 144, 16), 144), :]
        return dot(own, cp[:, cols]) + dot(other, pc[:, cols])

    left, right = slice(0, LEFT), slice(LEFT, INNER)

    def x_copy(k, src, dst, s, r):
        return pltpu.make_async_remote_copy(
            src_ref=src, dst_ref=dst.at[k], send_sem=s.at[k], recv_sem=r.at[k],
            device_id=((x + k + 1) % XS, me), device_id_type=MESH,
        )

    def y_copy(k, src, dst, s, r):
        return pltpu.make_async_remote_copy(
            src_ref=src, dst_ref=dst.at[k], send_sem=s.at[k], recv_sem=r.at[k],
            device_id=(x, seq(z, (y + k + 1) % YS, c)), device_id_type=MESH,
        )

    def first(k, p):
        if p == 0:
            return x_copy(k, gsx.at[k], grx, gsem_s.at[0], gsem_r.at[0])
        return y_copy(k, gsy.at[k], gry, gsem_s.at[1], gsem_r.at[1])

    def second(k, p):
        if p == 0:
            return y_copy(k, ys1.at[(y + k + 1) % YS], yr1, hsem_s.at[0], hsem_r.at[0])
        return x_copy(k, ys2.at[(x + k + 1) % XS], yr2, hsem_s.at[1], hsem_r.at[1])

    for k in range(3):
        gsx[k] = block((x + k + 1) % XS, left).astype(BF16)
        first(k, 0).start()
        gsy[k] = block((y + k + 1) % YS, right).astype(BF16)
        first(k, 1).start()
    gox[...] = block(x, left)
    goy[...] = block(y, right)

    def first_sum():
        for p, (own, got, out) in enumerate(((gox, grx, ys1), (goy, gry, ys2))):
            total = own[...]
            for k in range(3):
                first(k, p).wait()
                total = total + got[k].astype(F32)
            for d in range(4):
                out[d] = total[36 * d : 36 * d + 36].astype(BF16)
            for k in range(3):
                second(k, p).start()

    root1, root2 = seq(4 * c + x, y, c), seq(4 * c + y, x, c)
    z_copies = [
        pltpu.make_async_remote_copy(
            src_ref=src, dst_ref=dst.at[z], send_sem=zsem_s.at[p], recv_sem=zsem_r.at[p],
            device_id=(x, root), device_id_type=MESH,
        )
        for p, (src, dst, root) in enumerate(((zs1, zr1, root1), (zs2, zr2, root2)))
    ]
    is_root = (z == 4 * c + x, (y == x) & (z // 4 == c))

    def second_sum():
        for p, (mine, got, src, at, root, dst) in enumerate(
            ((ys1, yr1, zs1, y, root1, zr1), (ys2, yr2, zs2, x, root2, zr2))
        ):
            total = mine[at].astype(F32)
            for k in range(3):
                second(k, p).wait()
                total = total + got[k].astype(F32)
            src[...] = total.astype(BF16)

            @pl.when(root != me)
            def _():
                z_copies[p].start()

            @pl.when(root == me)
            def _():
                dst[z] = src[...]

    def b_copy(p, k, src, dst):
        dx, dc = OTHERS[k]
        return pltpu.make_async_remote_copy(
            src_ref=src.at[(c + dc) % CS], dst_ref=dst, send_sem=bsem_s.at[p, k], recv_sem=bsem_r.at[p],
            device_id=((x + dx) % XS, seq(z, y, (c + dc) % CS)), device_id_type=MESH,
        )

    parts = ((zr1, og1s, og1, root1), (zr2, og2s, og2, root2))

    def z_sum():
        for p, (got, out, dst, root) in enumerate(parts):

            @pl.when(is_root[p])
            def _():
                few, all_ = got.at[pl.ds(0, ZS - 1)], got

                @pl.when(root == me)
                def _():
                    pltpu.make_async_copy(few, few, zsem_r.at[p]).wait()

                @pl.when(root != me)
                def _():
                    pltpu.make_async_copy(all_, all_, zsem_r.at[p]).wait()

                total = got[0].astype(F32)
                for k in range(1, ZS):
                    total = total + got[k].astype(F32)
                out[0] = total[:18]
                out[1] = total[18:]
                for k in range(len(OTHERS)):
                    b_copy(p, k, out, dst).start()

    def last():
        for p, (got, out, dst, root) in enumerate(parts):
            cols = (left, right)[p]

            @pl.when(root != me)
            def _():
                z_copies[p].wait_send()

            @pl.when(is_root[p])
            def _():
                og_o[:, cols] = out[c]
                for k in range(len(OTHERS)):
                    b_copy(p, k, out, dst).wait_send()

            @pl.when(jnp.logical_not(is_root[p]))
            def _():
                b_copy(p, 0, out, dst).wait_recv()
                og_o[:, cols] = dst[...]


    @pl.loop(0, HEADS // GROUP)
    def _(n):
        rows = [
            pl.ds(pl.multiple_of(INNER * t + n * (GROUP * HD), 16), GROUP * HD) for t in range(3)
        ]
        for i in range(2):
            outs = ([], [], [])
            for t in range(GROUP):
                h = n * GROUP + t
                q, k, v = (qkvT[HEADS * u + h, :, lanes(i)] for u in range(3))
                g = gaT[h, :, lanes(i)]
                w = w32s[i, h]
                dw = dot(v, g, TN)
                ds = (w * (dw - jnp.sum(w * dw, axis=0, keepdims=True)) * SCALE).astype(BF16)
                outs[0].append(dot(k, ds))
                outs[1].append(dot(q, ds, NT))
                outs[2].append(dot(g, w.astype(BF16), NT))
            for u in range(3):
                gpT[rows[u], lanes(i)] = jnp.concatenate(outs[u], axis=0).astype(BF16)

    first_sum()

    @pl.loop(0, 2)
    def _(n):
        rows = pl.ds(pl.multiple_of(n * 576, 16), 576)
        glatT[rows, :] = dot(inw[rows, :], gpT[...]).astype(BF16)

    gs[...] = dot(to_frame, glatT[...], NT).astype(BF16).reshape(SEQ, 4, INNER)
    second_sum()
    exchange(3, gs, glat_o)
    z_sum()
    last()
    sent(0, xs)
    sent(1, cs)
    sent(2, ms)
    sent(3, gs)
    arrived(2, ms, mixed_o)
    arrived(3, gs, glat_o)


def unpack(mixed, glat, og, mixed_o, glat_o, og_o):
    mixed_o[0, 0] = mixed[...].reshape(256, INNER)
    glat_o[0, 0] = glat[...].reshape(256, INNER)
    og_o[...] = og[...]


def body(latents, in_weight, out_weight, cotangent, clip_lengths):
    width = latents.shape[3]
    vmem = pl.BlockSpec(memory_space=pltpu.VMEM)
    hbm = pl.BlockSpec(memory_space=pl.ANY)
    msg = (SEQ, 4, INNER)
    tok = (256, INNER)
    dma = pltpu.SemaphoreType.DMA
    mixed, grad_latents, out_grad = pl.pallas_call(
        kernel,
        out_shape=[
            jax.ShapeDtypeStruct(msg, BF16),
            jax.ShapeDtypeStruct(msg, BF16),
            jax.ShapeDtypeStruct((18, INNER), F32),
        ],
        in_specs=[hbm, hbm, pl.BlockSpec(memory_space=pltpu.SMEM), hbm, hbm],
        out_specs=[hbm, hbm, vmem],
        scratch_shapes=[pltpu.VMEM(tok, BF16)] * 2
        + [pltpu.VMEM(msg, BF16)] * 6
        + [
            pltpu.VMEM((INNER, 3 * INNER), BF16),
            pltpu.VMEM((3 * INNER, INNER), BF16),
            pltpu.VMEM((INNER, INNER), BF16),
            pltpu.VMEM((3 * HEADS, HD, 256), BF16),
            pltpu.VMEM((2, HEADS, 128, 128), F32),
            pltpu.VMEM((INNER, 256), BF16),
            pltpu.VMEM(tok, BF16),
            pltpu.VMEM((HEADS, HD, 256), BF16),
            pltpu.VMEM((3 * INNER, 256), BF16),
            pltpu.VMEM((INNER, 256), BF16),
            pltpu.VMEM((576, 256), BF16),
            pltpu.VMEM(tok, BF16),
            pltpu.VMEM((3, 144, LEFT), BF16),
            pltpu.VMEM((3, 144, LEFT), BF16),
            pltpu.VMEM((3, 144, RIGHT), BF16),
            pltpu.VMEM((3, 144, RIGHT), BF16),
            pltpu.VMEM((144, LEFT), F32),
            pltpu.VMEM((144, RIGHT), F32),
            pltpu.VMEM((4, 36, LEFT), BF16),
            pltpu.VMEM((3, 36, LEFT), BF16),
            pltpu.VMEM((4, 36, RIGHT), BF16),
            pltpu.VMEM((3, 36, RIGHT), BF16),
            pltpu.VMEM((36, LEFT), BF16),
            pltpu.VMEM((ZS, 36, LEFT), BF16),
            pltpu.VMEM((36, RIGHT), BF16),
            pltpu.VMEM((ZS, 36, RIGHT), BF16),
            pltpu.VMEM((2, 18, LEFT), F32),
            pltpu.VMEM((2, 18, RIGHT), F32),
            pltpu.VMEM((18, LEFT), F32),
            pltpu.VMEM((18, RIGHT), F32),
            pltpu.VMEM((128, 128), F32),
            dma((4,)), dma((4,)), dma((4,)), dma((4,)), dma((2,)), dma((2,)),
            dma((2, 3)), dma((2, 3)), dma((2, 3)), dma((2, 3)), dma((2,)), dma((2,)),
            dma((2, 7)), dma((2,)),
        ],
        compiler_params=pltpu.CompilerParams(
            collective_id=0, has_side_effects=True, vmem_limit_bytes=52 << 20
        ),
        name="sublayer",
    )(
        latents.reshape(256, width), cotangent.reshape(256, width), clip_lengths, in_weight, out_weight,
    )
    return pl.pallas_call(
        unpack,
        out_shape=[
            jax.ShapeDtypeStruct(latents.shape, BF16),
            jax.ShapeDtypeStruct(latents.shape, BF16),
            jax.ShapeDtypeStruct((18, INNER), F32),
        ],
        in_specs=[vmem] * 3,
        out_specs=[vmem] * 3,
        compiler_params=pltpu.CompilerParams(vmem_limit_bytes=8 << 20),
        name="unpack",
    )(mixed, grad_latents, out_grad)


def solution(mesh):
    placed = (P("dp", "seq", None, None), P(), P(), P("dp", "seq", None, None), P("dp", None))
    return jax.shard_map(
        body,
        mesh=mesh,
        in_specs=placed,
        out_specs=(P("dp", "seq", None, None), P("dp", "seq", None, None), P("seq", None)),
        check_vma=False,
    )
```

```python
import jax
import jax.numpy as jnp
from jax import lax
from jax.experimental import pallas as pl
from jax.experimental.pallas import tpu as pltpu
from jax.sharding import PartitionSpec as P

MESH = pl.DeviceIdType.MESH
BF16 = jnp.bfloat16
F32 = jnp.float32
HEADS, HD = 16, 72
INNER = HEADS * HD
ZS, YS, CS, XS = 8, 4, 2, 4
SEQ = ZS * YS * CS
SCALE = float(HD) ** -0.5
LOG2E = 1.4426950408889634
PARTS = (384, 768, 1152)
COLS = [slice(a, b) for a, b in zip((0,) + PARTS, PARTS)]
WIDTHS = [c.stop - c.start for c in COLS]
NP = len(PARTS)
NT = (((1,), (1,)), ((), ()))
NN = (((1,), (0,)), ((), ()))
TN = (((0,), (0,)), ((), ()))
OTHERS = [(dx, dc) for dx in range(XS) for dc in range(CS) if (dx, dc) != (0, 0)]
GROUP = 4
BATCH = 9


def dot(a, b, dims=NN):
    return lax.dot_general(a, b, dims, preferred_element_type=F32)


def kernel(*refs):
    lat_hbm, cot_hbm, len_ref, inw_hbm, outw_hbm, mixed_o, glat_o, og_o = refs[:8]
    (
        latv, cotv, xs, xr, ms, gs, inw, inwT, outw, qkvT, w32s, attT, cp, gaT, gpT, glatT, paT, pc,
        zs, zr, ogs, ogr, amask,
    ) = refs[8:31]
    (
        wsem, lsem, ssem, rsem, psem_s, psem_r, gsem_s, gsem_r, hsem_s, hsem_r,
        zsem_s, zsem_r, bsem_s, bsem_r,
    ) = refs[31:45]
    csp, crp, gsp, grp, gop, hsp, hrp = (refs[45 + NP * i : 45 + NP * i + NP] for i in range(7))
    x = lax.axis_index("dp")
    me = lax.axis_index("seq")
    z, y, c = me // (YS * CS), me // CS % YS, me % CS

    def seq(zz, yy, cc):
        return zz * (YS * CS) + yy * CS + cc

    loads = [
        pltpu.make_async_copy(s, d, wsem.at[k])
        for k, (s, d) in enumerate(((lat_hbm, latv), (cot_hbm, cotv), (inw_hbm, inw), (outw_hbm, outw)))
    ]
    for t in loads:
        t.start()

    def peer(i, r):
        dz = 4 + i // 2 - i % 2 * i
        return seq((z + dz) % ZS, (y + r // CS) % YS, (c + r) % CS)

    barrier = pltpu.get_barrier_semaphore()

    @pl.loop(0, SEQ - 1, unroll=9)
    def _(j):
        pl.semaphore_signal(barrier, inc=1, device_id=(x, peer(j // 8, 7 - j % 8)), device_id_type=MESH)

    for dx, dc in OTHERS[1:]:
        pl.semaphore_signal(
            barrier, inc=1, device_id=((x + dx) % XS, seq(z, y, (c + dc) % CS)), device_id_type=MESH
        )

    loads[0].wait()
    xs[...] = latv[...].reshape(SEQ, 4, INNER)
    pl.semaphore_wait(barrier, SEQ - 1 + len(OTHERS) - 1)

    def batch(k, src, dst, b, size=BATCH, sem=0):
        @pl.loop(0, size, unroll=9)
        def _(j):
            n = b * BATCH + j
            d = peer(n % 8, 7 - n // 8)
            pltpu.make_async_remote_copy(
                src_ref=src.at[d], dst_ref=dst.at[me], send_sem=ssem.at[k, sem], recv_sem=rsem.at[k],
                device_id=(x, d), device_id_type=MESH,
            ).start()

    def keep(k, src, dst):
        return pltpu.make_async_copy(src.at[me], dst.at[me], lsem.at[k])

    def exchange(k, src, dst):
        batch(k, src, dst, 0, SEQ - 1)
        keep(k, src, dst).start()

    def arrived(k, src, dst):
        keep(k, src, dst).wait()
        part = dst.at[pl.ds(0, SEQ - 1)]
        pltpu.make_async_copy(part, part, rsem.at[k]).wait()

    def sent(k, src, sem=0, size=SEQ - 1):
        part = src.at[pl.ds(0, size)]
        pltpu.make_async_copy(part, part, ssem.at[k, sem]).wait()

    exchange(0, xs, xr)
    loads[1].wait()
    for p in range(NP):
        csp[p][...] = cotv[:, COLS[p]].reshape(SEQ, 4, WIDTHS[p])

    r_i = lax.broadcasted_iota(jnp.int32, (256, 256), 0)
    c_i = lax.broadcasted_iota(jnp.int32, (256, 256), 1)
    to_patch = (c_i == r_i % SEQ * 4 + r_i // SEQ).astype(BF16)
    to_frame = (r_i == c_i % SEQ * 4 + c_i // SEQ).astype(BF16)

    ends = [len_ref[0, 0]]
    for i in range(1, 4):
        ends.append(ends[-1] + len_ref[0, i])
    rows2 = lax.broadcasted_iota(jnp.int32, (128, 128), 0)
    cols2 = lax.broadcasted_iota(jnp.int32, (128, 128), 1)

    def clip_of(frame):
        total = jnp.zeros_like(frame)
        for e in ends:
            total = total + (frame >= e).astype(jnp.int32)
        return total

    same = (rows2 // SEQ == cols2 // SEQ) & (clip_of(rows2 % SEQ) == clip_of(cols2 % SEQ))
    amask[...] = jnp.where(same, 0.0, -jnp.inf).astype(F32)

    loads[2].wait()

    @pl.loop(0, 9)
    def _(n):
        cols = pl.ds(pl.multiple_of(n * 384, 128), 384)
        inwT[cols, :] = inw[:, cols].T

    for p in range(NP):
        exchange(3 + p, csp[p], crp[p])
    loads[3].wait()

    arrived(0, xs, xr)
    xp = dot(to_patch, xr[...].reshape(256, INNER)).astype(BF16)

    @pl.loop(0, 6)
    def _(n):
        out = dot(inwT[pl.ds(pl.multiple_of(n * 576, 16), 576), :], xp, NT)
        for i in range(8):
            qkvT[n * 8 + i] = out[HD * i : HD * i + HD].astype(BF16)


    def lanes(i):
        return slice(128 * i, 128 * i + 128)

    @pl.loop(0, HEADS // GROUP)
    def _(n):
        for i in range(2):
            outs = []
            for t in range(GROUP):
                h = n * GROUP + t
                s = dot(qkvT[HEADS + h, :, lanes(i)], qkvT[h, :, lanes(i)], TN) + amask[...]
                e = jnp.exp2((s - jnp.max(s, axis=0, keepdims=True)) * (SCALE * LOG2E))
                w = e / jnp.sum(e, axis=0, keepdims=True)
                w32s[i, h] = w
                outs.append(dot(qkvT[2 * HEADS + h, :, lanes(i)], w.astype(BF16)))
            rows = pl.ds(pl.multiple_of(n * (GROUP * HD), 16), GROUP * HD)
            attT[rows, lanes(i)] = jnp.concatenate(outs, axis=0).astype(BF16)

    mate = seq(z, y, 1 - c)
    theirs = pl.ds(pl.multiple_of((1 - c) * 576, 16), 576)

    def to_mate(k, src, dst):
        return pltpu.make_async_remote_copy(
            src_ref=src, dst_ref=dst, send_sem=psem_s.at[k], recv_sem=psem_r.at[k],
            device_id=(x, mate), device_id_type=MESH,
        )

    att_copy = to_mate(0, attT.at[theirs], paT)
    cot_copies = [to_mate(1 + p, cp.at[:, COLS[p]], pc.at[:, COLS[p]]) for p in range(NP)]
    att_copy.start()

    def block(j, cols):
        own = attT[pl.ds(pl.multiple_of(c * 576 + j * 144, 16), 144), :]
        other = paT[pl.ds(pl.multiple_of(j * 144, 16), 144), :]
        return dot(own, cp[:, cols]) + dot(other, pc[:, cols])

    def x_copy(k, src, dst, s, r):
        return pltpu.make_async_remote_copy(
            src_ref=src, dst_ref=dst.at[k], send_sem=s.at[k], recv_sem=r.at[k],
            device_id=((x + k + 1) % XS, me), device_id_type=MESH,
        )

    def y_copy(k, src, dst, s, r):
        return pltpu.make_async_remote_copy(
            src_ref=src, dst_ref=dst.at[k], send_sem=s.at[k], recv_sem=r.at[k],
            device_id=(x, seq(z, (y + k + 1) % YS, c)), device_id_type=MESH,
        )

    def first(k, p):
        return x_copy(k, gsp[p].at[k], grp[p], gsem_s.at[p], gsem_r.at[p])

    def second(k, p):
        return y_copy(k, hsp[p].at[(y + k + 1) % YS], hrp[p], hsem_s.at[p], hsem_r.at[p])

    def cot_part(p):
        arrived(3 + p, csp[p], crp[p])
        cp[:, COLS[p]] = dot(to_patch, crp[p][...].reshape(256, WIDTHS[p])).astype(BF16)
        cot_copies[p].start()

    def blocks(p):
        cot_copies[p].wait()
        for k in range(3):
            gsp[p][k] = block((x + k + 1) % XS, COLS[p]).astype(BF16)
            first(k, p).start()
        gop[p][...] = block(x, COLS[p])

    cot_part(0)
    att_f = dot(to_frame, attT[...], NT).astype(BF16)
    ms[...] = dot(att_f, outw[...]).astype(BF16).reshape(SEQ, 4, INNER)
    att_copy.wait()
    keep(1, ms, mixed_o).start()
    blocks(0)
    cot_part(1)
    batch(1, ms, mixed_o, 0)
    blocks(1)
    cot_part(2)
    batch(1, ms, mixed_o, 1)

    @pl.loop(0, 2)
    def _(n):
        out = dot(outw[pl.ds(pl.multiple_of(n * 576, 16), 576), :], cp[...], NT)
        for i in range(8):
            gaT[n * 8 + i] = out[HD * i : HD * i + HD].astype(BF16)

    blocks(2)
    batch(1, ms, mixed_o, 2)

    def first_sum(p):
        total = gop[p][...]
        for k in range(3):
            first(k, p).wait()
            total = total + grp[p][k].astype(F32)
        for d in range(4):
            hsp[p][d] = total[36 * d : 36 * d + 36].astype(BF16)
        for k in range(3):
            second(k, p).start()

    root = seq(4 * c + x, y, c)
    z_copy = pltpu.make_async_remote_copy(
        src_ref=zs, dst_ref=zr.at[z], send_sem=zsem_s, recv_sem=zsem_r,
        device_id=(x, root), device_id_type=MESH,
    )

    def second_sum():
        for p in range(NP):
            total = hsp[p][y].astype(F32)
            for k in range(3):
                second(k, p).wait()
                total = total + hrp[p][k].astype(F32)
            zs[:, COLS[p]] = total.astype(BF16)

        @pl.when(root != me)
        def _():
            z_copy.start()

        @pl.when(root == me)
        def _():
            zr[z] = zs[...]

    def b_copy(k):
        dx, dc = OTHERS[k]
        return pltpu.make_async_remote_copy(
            src_ref=ogs.at[(c + dc) % CS], dst_ref=ogr, send_sem=bsem_s.at[k], recv_sem=bsem_r,
            device_id=((x + dx) % XS, seq(z, y, (c + dc) % CS)), device_id_type=MESH,
        )

    def z_sum():
        @pl.when(root == me)
        def _():
            part = zr.at[pl.ds(0, ZS - 1)]
            pltpu.make_async_copy(part, part, zsem_r).wait()
            total = zr[0].astype(F32)
            for k in range(1, ZS):
                total = total + zr[k].astype(F32)
            ogs[0] = total[:18].astype(ogs.dtype)
            ogs[1] = total[18:].astype(ogs.dtype)
            for k in range(len(OTHERS)):
                b_copy(k).start()

    def last():
        @pl.when(root == me)
        def _():
            og_o[...] = ogs[c].astype(F32)
            for k in range(len(OTHERS)):
                b_copy(k).wait_send()

        @pl.when(root != me)
        def _():
            z_copy.wait_send()
            b_copy(0).wait_recv()
            og_o[...] = ogr[...].astype(F32)

    def backward(n):
        rows = [
            pl.ds(pl.multiple_of(INNER * t + n * (GROUP * HD), 16), GROUP * HD) for t in range(3)
        ]
        for i in range(2):
            outs = ([], [], [])
            for t in range(GROUP):
                h = n * GROUP + t
                q, k, v = (qkvT[HEADS * u + h, :, lanes(i)] for u in range(3))
                g = gaT[h, :, lanes(i)]
                w = w32s[i, h]
                dw = dot(v, g, TN)
                ds = (w * (dw - jnp.sum(w * dw, axis=0, keepdims=True)) * SCALE).astype(BF16)
                outs[0].append(dot(k, ds))
                outs[1].append(dot(q, ds, NT))
                outs[2].append(dot(g, w.astype(BF16), NT))
            for u in range(3):
                gpT[rows[u], lanes(i)] = jnp.concatenate(outs[u], axis=0).astype(BF16)
        batch(1, ms, mixed_o, n + 3)

    pl.loop(0, HEADS // GROUP)(backward)
    first_sum(0)
    first_sum(1)

    @pl.loop(0, 2)
    def _(n):
        rows = pl.ds(pl.multiple_of(n * 576, 16), 576)
        glatT[rows, :] = dot(inw[rows, :], gpT[...]).astype(BF16)

    first_sum(2)
    gs[...] = dot(to_frame, glatT[...], NT).astype(BF16).reshape(SEQ, 4, INNER)
    batch(2, gs, glat_o, 0, 18)
    second_sum()
    batch(2, gs, glat_o, 18 // BATCH, SEQ - 1 - 18)
    keep(2, gs, glat_o).start()
    z_sum()
    last()
    sent(0, xs)
    for p in range(NP):
        sent(3 + p, csp[p])
    sent(1, ms)
    sent(2, gs)
    arrived(1, ms, mixed_o)
    arrived(2, gs, glat_o)


def unpack(mixed, glat, og, mixed_o, glat_o, og_o):
    mixed_o[0, 0] = mixed[...].reshape(256, INNER)
    glat_o[0, 0] = glat[...].reshape(256, INNER)
    og_o[...] = og[...]


def body(latents, in_weight, out_weight, cotangent, clip_lengths):
    width = latents.shape[3]
    vmem = pl.BlockSpec(memory_space=pltpu.VMEM)
    hbm = pl.BlockSpec(memory_space=pl.ANY)
    msg = (SEQ, 4, INNER)
    tok = (256, INNER)
    dma = pltpu.SemaphoreType.DMA
    mixed, grad_latents, out_grad = pl.pallas_call(
        kernel,
        out_shape=[
            jax.ShapeDtypeStruct(msg, BF16),
            jax.ShapeDtypeStruct(msg, BF16),
            jax.ShapeDtypeStruct((18, INNER), F32),
        ],
        in_specs=[hbm, hbm, pl.BlockSpec(memory_space=pltpu.SMEM), hbm, hbm],
        out_specs=[hbm, hbm, vmem],
        scratch_shapes=[pltpu.VMEM(tok, BF16)] * 2
        + [pltpu.VMEM(msg, BF16)] * 4
        + [
            pltpu.VMEM((INNER, 3 * INNER), BF16),
            pltpu.VMEM((3 * INNER, INNER), BF16),
            pltpu.VMEM((INNER, INNER), BF16),
            pltpu.VMEM((3 * HEADS, HD, 256), BF16),
            pltpu.VMEM((2, HEADS, 128, 128), F32),
            pltpu.VMEM((INNER, 256), BF16),
            pltpu.VMEM(tok, BF16),
            pltpu.VMEM((HEADS, HD, 256), BF16),
            pltpu.VMEM((3 * INNER, 256), BF16),
            pltpu.VMEM((INNER, 256), BF16),
            pltpu.VMEM((576, 256), BF16),
            pltpu.VMEM(tok, BF16),
            pltpu.VMEM((36, INNER), BF16),
            pltpu.VMEM((ZS, 36, INNER), BF16),
            pltpu.VMEM((2, 18, INNER), BF16),
            pltpu.VMEM((18, INNER), BF16),
            pltpu.VMEM((128, 128), F32),
            dma((4,)), dma((3 + NP,)), dma((3 + NP, 1)), dma((3 + NP,)), dma((1 + NP,)), dma((1 + NP,)),
            dma((NP, 3)), dma((NP, 3)), dma((NP, 3)), dma((NP, 3)), dma, dma,
            dma((7,)), dma,
        ]
        + [pltpu.VMEM((SEQ, 4, w), BF16) for w in WIDTHS] * 2
        + [pltpu.VMEM((3, 144, w), BF16) for w in WIDTHS] * 2
        + [pltpu.VMEM((144, w), F32) for w in WIDTHS]
        + [pltpu.VMEM((4, 36, w), BF16) for w in WIDTHS]
        + [pltpu.VMEM((3, 36, w), BF16) for w in WIDTHS],
        compiler_params=pltpu.CompilerParams(
            collective_id=0, has_side_effects=True, vmem_limit_bytes=52 << 20
        ),
        name="sublayer",
    )(
        latents.reshape(256, width), cotangent.reshape(256, width), clip_lengths, in_weight, out_weight,
    )
    return pl.pallas_call(
        unpack,
        out_shape=[
            jax.ShapeDtypeStruct(latents.shape, BF16),
            jax.ShapeDtypeStruct(latents.shape, BF16),
            jax.ShapeDtypeStruct((18, INNER), F32),
        ],
        in_specs=[vmem] * 3,
        out_specs=[vmem] * 3,
        compiler_params=pltpu.CompilerParams(vmem_limit_bytes=8 << 20),
        name="unpack",
    )(mixed, grad_latents, out_grad)


def solution(mesh):
    placed = (P("dp", "seq", None, None), P(), P(), P("dp", "seq", None, None), P("dp", None))
    return jax.shard_map(
        body,
        mesh=mesh,
        in_specs=placed,
        out_specs=(P("dp", "seq", None, None), P("dp", "seq", None, None), P("seq", None)),
        check_vma=False,
    )
```

```python
import jax
import jax.numpy as jnp
from jax import lax
from jax.experimental import pallas as pl
from jax.experimental.pallas import tpu as pltpu
from jax.sharding import PartitionSpec as P

MESH = pl.DeviceIdType.MESH
BF16 = jnp.bfloat16
F32 = jnp.float32
HEADS, HD = 16, 72
INNER = HEADS * HD
ZS, YS, CS, XS = 8, 4, 2, 4
SEQ = ZS * YS * CS
SCALE = float(HD) ** -0.5
LOG2E = 1.4426950408889634
PARTS = (384, 768, 1152)
COLS = [slice(a, b) for a, b in zip((0,) + PARTS, PARTS)]
WIDTHS = [c.stop - c.start for c in COLS]
NP = len(PARTS)
NT = (((1,), (1,)), ((), ()))
NN = (((1,), (0,)), ((), ()))
TN = (((0,), (0,)), ((), ()))
OTHERS = [(dx, dc) for dx in range(XS) for dc in range(CS) if (dx, dc) != (0, 0)]
GROUP = 4
BATCH = 9


def dot(a, b, dims=NN):
    return lax.dot_general(a, b, dims, preferred_element_type=F32)


def kernel(*refs):
    lat_hbm, cot_hbm, len_ref, inw_hbm, outw_hbm, mixed_o, glat_o, og_o = refs[:8]
    (
        latv, cotv, xs, xr, ms, gs, inw, inwT, outw, qkvT, w32s, attT, cp, gaT, gpT, glatT, paT, pc,
        amask,
    ) = refs[8:27]
    (
        wsem, lsem, ssem, rsem, psem_s, psem_r, gsem_s, gsem_r, hsem_s, hsem_r,
        zsem_s, zsem_r, bsem_s, bsem_r,
    ) = refs[27:41]
    csp, crp, gsp, grp, gop, hsp, hrp, zsp, zrp, ogsp, ogrp = (
        refs[41 + NP * i : 41 + NP * i + NP] for i in range(11)
    )
    x = lax.axis_index("dp")
    me = lax.axis_index("seq")
    z, y, c = me // (YS * CS), me // CS % YS, me % CS

    def seq(zz, yy, cc):
        return zz * (YS * CS) + yy * CS + cc

    loads = [
        pltpu.make_async_copy(s, d, wsem.at[k])
        for k, (s, d) in enumerate(((lat_hbm, latv), (cot_hbm, cotv), (inw_hbm, inw), (outw_hbm, outw)))
    ]
    for t in loads:
        t.start()

    def peer(i, r):
        dz = 4 + i // 2 - i % 2 * i
        return seq((z + dz) % ZS, (y + r // CS) % YS, (c + r) % CS)

    barrier = pltpu.get_barrier_semaphore()

    @pl.loop(0, SEQ - 1, unroll=9)
    def _(j):
        pl.semaphore_signal(barrier, inc=1, device_id=(x, peer(j // 8, 7 - j % 8)), device_id_type=MESH)

    for dx, dc in OTHERS[1:]:
        pl.semaphore_signal(
            barrier, inc=1, device_id=((x + dx) % XS, seq(z, y, (c + dc) % CS)), device_id_type=MESH
        )

    loads[0].wait()
    xs[...] = latv[...].reshape(SEQ, 4, INNER)
    pl.semaphore_wait(barrier, SEQ - 1 + len(OTHERS) - 1)

    def batch(k, src, dst, b, size=BATCH, sem=0):
        @pl.loop(0, size, unroll=9)
        def _(j):
            n = b * BATCH + j
            d = peer(n % 8, 7 - n // 8)
            pltpu.make_async_remote_copy(
                src_ref=src.at[d], dst_ref=dst.at[me], send_sem=ssem.at[k, sem], recv_sem=rsem.at[k],
                device_id=(x, d), device_id_type=MESH,
            ).start()

    def keep(k, src, dst):
        return pltpu.make_async_copy(src.at[me], dst.at[me], lsem.at[k])

    def exchange(k, src, dst):
        batch(k, src, dst, 0, SEQ - 1)
        keep(k, src, dst).start()

    def arrived(k, src, dst):
        keep(k, src, dst).wait()
        part = dst.at[pl.ds(0, SEQ - 1)]
        pltpu.make_async_copy(part, part, rsem.at[k]).wait()

    def sent(k, src, sem=0, size=SEQ - 1):
        part = src.at[pl.ds(0, size)]
        pltpu.make_async_copy(part, part, ssem.at[k, sem]).wait()

    exchange(0, xs, xr)
    loads[1].wait()
    for p in range(NP):
        csp[p][...] = cotv[:, COLS[p]].reshape(SEQ, 4, WIDTHS[p])

    r_i = lax.broadcasted_iota(jnp.int32, (256, 256), 0)
    c_i = lax.broadcasted_iota(jnp.int32, (256, 256), 1)
    to_patch = (c_i == r_i % SEQ * 4 + r_i // SEQ).astype(BF16)
    to_frame = (r_i == c_i % SEQ * 4 + c_i // SEQ).astype(BF16)

    ends = [len_ref[0, 0]]
    for i in range(1, 4):
        ends.append(ends[-1] + len_ref[0, i])
    rows2 = lax.broadcasted_iota(jnp.int32, (128, 128), 0)
    cols2 = lax.broadcasted_iota(jnp.int32, (128, 128), 1)

    def clip_of(frame):
        total = jnp.zeros_like(frame)
        for e in ends:
            total = total + (frame >= e).astype(jnp.int32)
        return total

    same = (rows2 // SEQ == cols2 // SEQ) & (clip_of(rows2 % SEQ) == clip_of(cols2 % SEQ))
    amask[...] = jnp.where(same, 0.0, -jnp.inf).astype(F32)

    loads[2].wait()

    @pl.loop(0, 9)
    def _(n):
        cols = pl.ds(pl.multiple_of(n * 384, 128), 384)
        inwT[cols, :] = inw[:, cols].T

    for p in range(NP):
        exchange(3 + p, csp[p], crp[p])
    loads[3].wait()

    arrived(0, xs, xr)
    xp = dot(to_patch, xr[...].reshape(256, INNER)).astype(BF16)

    @pl.loop(0, 2)
    def _(n):
        out = dot(inwT[pl.ds(pl.multiple_of(n * 1728, 16), 1728), :], xp, NT)
        for i in range(24):
            qkvT[n * 24 + i] = out[HD * i : HD * i + HD].astype(BF16)


    def lanes(i):
        return slice(128 * i, 128 * i + 128)

    def diagonal(parts):
        zero = jnp.zeros((128, 128), BF16)
        top = jnp.concatenate([parts[0], zero], axis=1)
        return jnp.concatenate([top, jnp.concatenate([zero, parts[1]], axis=1)], axis=0)

    def group_rows(n, base=0):
        return pl.ds(pl.multiple_of(base + n * (GROUP * HD), 16), GROUP * HD)

    @pl.loop(0, HEADS // GROUP)
    def _(n):
        outs = []
        for t in range(GROUP):
            h = n * GROUP + t
            parts = []
            for i in range(2):
                s = dot(qkvT[HEADS + h, :, lanes(i)], qkvT[h, :, lanes(i)], TN) + amask[...]
                e = jnp.exp2((s - jnp.max(s, axis=0, keepdims=True)) * (SCALE * LOG2E))
                w = e / jnp.sum(e, axis=0, keepdims=True)
                w32s[i, h] = w
                parts.append(w.astype(BF16))
            outs.append(dot(qkvT[2 * HEADS + h], diagonal(parts)))
        attT[group_rows(n), :] = jnp.concatenate(outs, axis=0).astype(BF16)

    mate = seq(z, y, 1 - c)
    theirs = pl.ds(pl.multiple_of((1 - c) * 576, 16), 576)

    def to_mate(k, src, dst):
        return pltpu.make_async_remote_copy(
            src_ref=src, dst_ref=dst, send_sem=psem_s.at[k], recv_sem=psem_r.at[k],
            device_id=(x, mate), device_id_type=MESH,
        )

    att_copy = to_mate(0, attT.at[theirs], paT)
    cot_copies = [to_mate(1 + p, cp.at[:, COLS[p]], pc.at[:, COLS[p]]) for p in range(NP)]
    att_copy.start()

    def block(j, cols):
        own = attT[pl.ds(pl.multiple_of(c * 576 + j * 144, 16), 144), :]
        other = paT[pl.ds(pl.multiple_of(j * 144, 16), 144), :]
        return dot(own, cp[:, cols]) + dot(other, pc[:, cols])

    def x_copy(k, src, dst, s, r):
        return pltpu.make_async_remote_copy(
            src_ref=src, dst_ref=dst.at[k], send_sem=s.at[k], recv_sem=r.at[k],
            device_id=((x + k + 1) % XS, me), device_id_type=MESH,
        )

    def y_copy(k, src, dst, s, r):
        return pltpu.make_async_remote_copy(
            src_ref=src, dst_ref=dst.at[k], send_sem=s.at[k], recv_sem=r.at[k],
            device_id=(x, seq(z, (y + k + 1) % YS, c)), device_id_type=MESH,
        )

    def first(k, p):
        return x_copy(k, gsp[p].at[k], grp[p], gsem_s.at[p], gsem_r.at[p])

    def second(k, p):
        return y_copy(k, hsp[p].at[(y + k + 1) % YS], hrp[p], hsem_s.at[p], hsem_r.at[p])

    def cot_part(p):
        arrived(3 + p, csp[p], crp[p])
        cp[:, COLS[p]] = dot(to_patch, crp[p][...].reshape(256, WIDTHS[p])).astype(BF16)
        cot_copies[p].start()

    def blocks(p):
        cot_copies[p].wait()
        for k in range(3):
            gsp[p][k] = block((x + k + 1 + p) % XS, COLS[p]).astype(BF16)
            first(k, p).start()
        gop[p][...] = block((x + p) % XS, COLS[p])

    cot_part(0)
    att_f = dot(to_frame, attT[...], NT).astype(BF16)
    att_copy.wait()
    blocks(0)
    ms[...] = dot(att_f, outw[...]).astype(BF16).reshape(SEQ, 4, INNER)
    keep(1, ms, mixed_o).start()
    cot_part(1)
    batch(1, ms, mixed_o, 0)
    blocks(1)
    cot_part(2)
    batch(1, ms, mixed_o, 1)

    @pl.loop(0, 2)
    def _(n):
        out = dot(outw[pl.ds(pl.multiple_of(n * 576, 16), 576), :], cp[...], NT)
        for i in range(8):
            gaT[n * 8 + i] = out[HD * i : HD * i + HD].astype(BF16)

    blocks(2)
    batch(1, ms, mixed_o, 2)

    def first_sum(p):
        total = gop[p][...]
        for k in range(3):
            first(k, p).wait()
            total = total + grp[p][k].astype(F32)
        for d in range(4):
            hsp[p][d] = total[36 * d : 36 * d + 36].astype(BF16)
        for k in range(3):
            second(k, p).start()

    roots = [seq(4 * c + (x + p) % XS, y, c) for p in range(NP)]
    def z_copy(p):
        return pltpu.make_async_remote_copy(
            src_ref=zsp[p], dst_ref=zrp[p].at[z], send_sem=zsem_s.at[p], recv_sem=zsem_r.at[p],
            device_id=(x, roots[p]), device_id_type=MESH,
        )

    def second_sum(p):
        total = hsp[p][y].astype(F32)
        for k in range(3):
            second(k, p).wait()
            total = total + hrp[p][k].astype(F32)
        zsp[p][...] = total.astype(BF16)

        @pl.when(roots[p] != me)
        def _():
            z_copy(p).start()

        @pl.when(roots[p] == me)
        def _():
            zrp[p][z] = zsp[p][...]

    def b_copy(k, p):
        dx, dc = OTHERS[k]
        return pltpu.make_async_remote_copy(
            src_ref=ogsp[p].at[(c + dc) % CS], dst_ref=ogrp[p], send_sem=bsem_s.at[p, k], recv_sem=bsem_r.at[p],
            device_id=((x + dx) % XS, seq(z, y, (c + dc) % CS)), device_id_type=MESH,
        )

    def z_sum(p):
        @pl.when(roots[p] == me)
        def _():
            part = zrp[p].at[pl.ds(0, ZS - 1)]
            pltpu.make_async_copy(part, part, zsem_r.at[p]).wait()
            total = zrp[p][0].astype(F32)
            for k in range(1, ZS):
                total = total + zrp[p][k].astype(F32)
            ogsp[p][0] = total[:18].astype(BF16)
            ogsp[p][1] = total[18:].astype(BF16)
            for k in range(len(OTHERS)):
                b_copy(k, p).start()

    def last(p):
        @pl.when(roots[p] == me)
        def _():
            og_o[:, COLS[p]] = ogsp[p][c].astype(F32)
            for k in range(len(OTHERS)):
                b_copy(k, p).wait_send()

        @pl.when(roots[p] != me)
        def _():
            z_copy(p).wait_send()
            b_copy(0, p).wait_recv()
            og_o[:, COLS[p]] = ogrp[p][...].astype(F32)

    def backward(n):
        outs = ([], [], [])
        for t in range(GROUP):
            h = n * GROUP + t
            ws, ds = [], []
            for i in range(2):
                w = w32s[i, h]
                dw = dot(qkvT[2 * HEADS + h, :, lanes(i)], gaT[h, :, lanes(i)], TN)
                ds.append((w * (dw - jnp.sum(w * dw, axis=0, keepdims=True)) * SCALE).astype(BF16))
                ws.append(w.astype(BF16))
            ds = diagonal(ds)
            outs[0].append(dot(qkvT[HEADS + h], ds))
            outs[1].append(dot(qkvT[h], ds, NT))
            outs[2].append(dot(gaT[h], diagonal(ws), NT))
        for u in range(3):
            gpT[group_rows(n, INNER * u), :] = jnp.concatenate(outs[u], axis=0).astype(BF16)
    @pl.loop(0, 2)
    def _(n):
        backward(n)
        batch(1, ms, mixed_o, n + 3)

    first_sum(0)
    @pl.loop(2, 4)
    def _(n):
        backward(n)
        batch(1, ms, mixed_o, n + 3)

    first_sum(1)

    glatT[...] = dot(inw[...], gpT[...]).astype(BF16)

    gs[...] = dot(to_frame, glatT[...], NT).astype(BF16).reshape(SEQ, 4, INNER)
    first_sum(2)

    keep(2, gs, glat_o).start()
    batch(2, gs, glat_o, 0, 18)
    second_sum(0)
    second_sum(1)
    batch(2, gs, glat_o, 18 // BATCH, 9)
    second_sum(2)
    batch(2, gs, glat_o, (18 + 9) // BATCH, SEQ - 1 - 18 - 9)
    for p in range(NP):
        z_sum(p)
    for p in range(NP):
        last(p)
    sent(0, xs)
    for p in range(NP):
        sent(3 + p, csp[p])
    sent(1, ms)
    sent(2, gs)
    arrived(1, ms, mixed_o)
    arrived(2, gs, glat_o)


def unpack(mixed, glat, og, mixed_o, glat_o, og_o):
    mixed_o[0, 0] = mixed[...].reshape(256, INNER)
    glat_o[0, 0] = glat[...].reshape(256, INNER)
    og_o[...] = og[...]


def body(latents, in_weight, out_weight, cotangent, clip_lengths):
    width = latents.shape[3]
    vmem = pl.BlockSpec(memory_space=pltpu.VMEM)
    hbm = pl.BlockSpec(memory_space=pl.ANY)
    msg = (SEQ, 4, INNER)
    tok = (256, INNER)
    dma = pltpu.SemaphoreType.DMA
    mixed, grad_latents, out_grad = pl.pallas_call(
        kernel,
        out_shape=[
            jax.ShapeDtypeStruct(msg, BF16),
            jax.ShapeDtypeStruct(msg, BF16),
            jax.ShapeDtypeStruct((18, INNER), F32),
        ],
        in_specs=[hbm, hbm, pl.BlockSpec(memory_space=pltpu.SMEM), hbm, hbm],
        out_specs=[hbm, hbm, vmem],
        scratch_shapes=[pltpu.VMEM(tok, BF16)] * 2
        + [pltpu.VMEM(msg, BF16)] * 4
        + [
            pltpu.VMEM((INNER, 3 * INNER), BF16),
            pltpu.VMEM((3 * INNER, INNER), BF16),
            pltpu.VMEM((INNER, INNER), BF16),
            pltpu.VMEM((3 * HEADS, HD, 256), BF16),
            pltpu.VMEM((2, HEADS, 128, 128), F32),
            pltpu.VMEM((INNER, 256), BF16),
            pltpu.VMEM(tok, BF16),
            pltpu.VMEM((HEADS, HD, 256), BF16),
            pltpu.VMEM((3 * INNER, 256), BF16),
            pltpu.VMEM((INNER, 256), BF16),
            pltpu.VMEM((576, 256), BF16),
            pltpu.VMEM(tok, BF16),
            pltpu.VMEM((128, 128), F32),
            dma((4,)), dma((3 + NP,)), dma((3 + NP, 1)), dma((3 + NP,)), dma((1 + NP,)), dma((1 + NP,)),
            dma((NP, 3)), dma((NP, 3)), dma((NP, 3)), dma((NP, 3)), dma((NP,)), dma((NP,)),
            dma((NP, 7)), dma((NP,)),
        ]
        + [pltpu.VMEM((SEQ, 4, w), BF16) for w in WIDTHS] * 2
        + [pltpu.VMEM((3, 144, w), BF16) for w in WIDTHS] * 2
        + [pltpu.VMEM((144, w), F32) for w in WIDTHS]
        + [pltpu.VMEM((4, 36, w), BF16) for w in WIDTHS]
        + [pltpu.VMEM((3, 36, w), BF16) for w in WIDTHS]
        + [pltpu.VMEM((36, w), BF16) for w in WIDTHS]
        + [pltpu.VMEM((ZS, 36, w), BF16) for w in WIDTHS]
        + [pltpu.VMEM((2, 18, w), BF16) for w in WIDTHS]
        + [pltpu.VMEM((18, w), BF16) for w in WIDTHS],
        compiler_params=pltpu.CompilerParams(
            collective_id=0, has_side_effects=True, vmem_limit_bytes=52 << 20
        ),
        name="sublayer",
    )(
        latents.reshape(256, width), cotangent.reshape(256, width), clip_lengths, in_weight, out_weight,
    )
    return pl.pallas_call(
        unpack,
        out_shape=[
            jax.ShapeDtypeStruct(latents.shape, BF16),
            jax.ShapeDtypeStruct(latents.shape, BF16),
            jax.ShapeDtypeStruct((18, INNER), F32),
        ],
        in_specs=[vmem] * 3,
        out_specs=[vmem] * 3,
        compiler_params=pltpu.CompilerParams(vmem_limit_bytes=8 << 20),
        name="unpack",
    )(mixed, grad_latents, out_grad)


def solution(mesh):
    placed = (P("dp", "seq", None, None), P(), P(), P("dp", "seq", None, None), P("dp", None))
    return jax.shard_map(
        body,
        mesh=mesh,
        in_specs=placed,
        out_specs=(P("dp", "seq", None, None), P("dp", "seq", None, None), P("seq", None)),
        check_vma=False,
    )
```

```python
import jax
import jax.numpy as jnp
from jax import lax
from jax.experimental import pallas as pl
from jax.experimental.pallas import tpu as pltpu
from jax.sharding import PartitionSpec as P

MESH = pl.DeviceIdType.MESH
BF16 = jnp.bfloat16
F32 = jnp.float32
HEADS, HD = 16, 72
INNER = HEADS * HD
ZS, YS, CS, XS = 8, 4, 2, 4
SEQ = ZS * YS * CS
SCALE = float(HD) ** -0.5
LOG2E = 1.4426950408889634
PARTS = (384, 768, 1152)
COLS = [slice(a, b) for a, b in zip((0,) + PARTS, PARTS)]
WIDTHS = [c.stop - c.start for c in COLS]
NP = len(PARTS)
NT = (((1,), (1,)), ((), ()))
NN = (((1,), (0,)), ((), ()))
TN = (((0,), (0,)), ((), ()))
OTHERS = [(dx, dc) for dx in range(XS) for dc in range(CS) if (dx, dc) != (0, 0)]
GROUP = 4
BATCH = 9


def dot(a, b, dims=NN):
    return lax.dot_general(a, b, dims, preferred_element_type=F32)


def kernel(*refs):
    lat_hbm, cot_hbm, len_hbm, inw_hbm, outw_hbm, mixed_o, glat_o, og_hbm = refs[:8]
    (
        latv, cotv, xs, xr, ms, gs, inw, inwT, outw, qkvT, w32s, attT, cp, gaT, gpT, glatT, paT, pc,
        amask, og_o, len_ref,
    ) = refs[8:29]
    (
        wsem, lsem, ssem, rsem, psem_s, psem_r, gsem_s, gsem_r, hsem_s, hsem_r,
        zsem_s, zsem_r, bsem_s, bsem_r,
    ) = refs[29:43]
    csp, crp, gsp, grp, gop, hsp, hrp, zsp, zrp, ogsp, ogrp = (
        refs[43 + NP * i : 43 + NP * i + NP] for i in range(11)
    )
    x = lax.axis_index("dp")
    me = lax.axis_index("seq")
    z, y, c = me // (YS * CS), me // CS % YS, me % CS

    def seq(zz, yy, cc):
        return zz * (YS * CS) + yy * CS + cc

    loads = [
        pltpu.make_async_copy(s, d, wsem.at[k])
        for k, (s, d) in enumerate(((lat_hbm, latv), (cot_hbm, cotv), (inw_hbm, inw), (outw_hbm, outw), (len_hbm, len_ref)))
    ]
    for t in loads:
        t.start()

    def peer(i, r):
        dz = 4 + i // 2 - i % 2 * i
        return seq((z + dz) % ZS, (y + r // CS) % YS, (c + r) % CS)

    barrier = pltpu.get_barrier_semaphore()

    @pl.loop(0, SEQ - 1, unroll=9)
    def _(j):
        pl.semaphore_signal(barrier, inc=1, device_id=(x, peer(j // 8, 7 - j % 8)), device_id_type=MESH)

    for dx, dc in OTHERS[1:]:
        pl.semaphore_signal(
            barrier, inc=1, device_id=((x + dx) % XS, seq(z, y, (c + dc) % CS)), device_id_type=MESH
        )

    loads[0].wait()
    xs[...] = latv[...].reshape(SEQ, 4, INNER)
    pl.semaphore_wait(barrier, SEQ - 1 + len(OTHERS) - 1)

    def batch(k, src, dst, b, size=BATCH, sem=0):
        @pl.loop(0, size, unroll=9)
        def _(j):
            n = b * BATCH + j
            if k == 2:
                n = n + (n + 56) // 63
                d = peer(n % 8, n // 8)
            else:
                d = peer(n % 8, 7 - n // 8)
            pltpu.make_async_remote_copy(
                src_ref=src.at[d], dst_ref=dst.at[me], send_sem=ssem.at[k, sem], recv_sem=rsem.at[k],
                device_id=(x, d), device_id_type=MESH,
            ).start()

    def keep(k, src, dst):
        return pltpu.make_async_copy(src.at[me], dst.at[me], lsem.at[k])

    def exchange(k, src, dst):
        batch(k, src, dst, 0, SEQ - 1)
        keep(k, src, dst).start()

    def arrived(k, src, dst):
        keep(k, src, dst).wait()
        part = dst.at[pl.ds(0, SEQ - 1)]
        pltpu.make_async_copy(part, part, rsem.at[k]).wait()

    def sent(k, src, sem=0, size=SEQ - 1):
        part = src.at[pl.ds(0, size)]
        pltpu.make_async_copy(part, part, ssem.at[k, sem]).wait()

    exchange(0, xs, xr)
    loads[1].wait()
    for p in range(NP):
        csp[p][...] = cotv[:, COLS[p]].reshape(SEQ, 4, WIDTHS[p])

    r_i = lax.broadcasted_iota(jnp.int32, (256, 256), 0)
    c_i = lax.broadcasted_iota(jnp.int32, (256, 256), 1)
    to_patch = (c_i == r_i % SEQ * 4 + r_i // SEQ).astype(BF16)
    to_frame = (r_i == c_i % SEQ * 4 + c_i // SEQ).astype(BF16)

    loads[4].wait()
    ends = [len_ref[0, 0]]
    for i in range(1, 4):
        ends.append(ends[-1] + len_ref[0, i])
    rows2 = lax.broadcasted_iota(jnp.int32, (128, 128), 0)
    cols2 = lax.broadcasted_iota(jnp.int32, (128, 128), 1)

    def clip_of(frame):
        total = jnp.zeros_like(frame)
        for e in ends:
            total = total + (frame >= e).astype(jnp.int32)
        return total

    same = (rows2 // SEQ == cols2 // SEQ) & (clip_of(rows2 % SEQ) == clip_of(cols2 % SEQ))
    amask[...] = jnp.where(same, 0.0, -jnp.inf).astype(F32)

    loads[2].wait()

    @pl.loop(0, 9)
    def _(n):
        cols = pl.ds(pl.multiple_of(n * 384, 128), 384)
        inwT[cols, :] = inw[:, cols].T

    for p in range(NP):
        exchange(3 + p, csp[p], crp[p])
    loads[3].wait()

    arrived(0, xs, xr)
    xp = dot(to_patch, xr[...].reshape(256, INNER)).astype(BF16)

    @pl.loop(0, 2)
    def _(n):
        out = dot(inwT[pl.ds(pl.multiple_of(n * 1728, 16), 1728), :], xp, NT)
        for i in range(24):
            qkvT[n * 24 + i] = out[HD * i : HD * i + HD].astype(BF16)


    def lanes(i):
        return slice(128 * i, 128 * i + 128)

    def diagonal(parts):
        zero = jnp.zeros((128, 128), BF16)
        top = jnp.concatenate([parts[0], zero], axis=1)
        return jnp.concatenate([top, jnp.concatenate([zero, parts[1]], axis=1)], axis=0)

    def group_rows(n, base=0):
        return pl.ds(pl.multiple_of(base + n * (GROUP * HD), 16), GROUP * HD)

    @pl.loop(0, HEADS // GROUP)
    def _(n):
        outs = []
        for t in range(GROUP):
            h = n * GROUP + t
            parts = []
            for i in range(2):
                s = dot(qkvT[HEADS + h, :, lanes(i)], qkvT[h, :, lanes(i)], TN) + amask[...]
                e = jnp.exp2((s - jnp.max(s, axis=0, keepdims=True)) * (SCALE * LOG2E))
                w = e / jnp.sum(e, axis=0, keepdims=True)
                w32s[i, h] = w
                parts.append(w.astype(BF16))
            outs.append(dot(qkvT[2 * HEADS + h], diagonal(parts)))
        attT[group_rows(n), :] = jnp.concatenate(outs, axis=0).astype(BF16)

    mate = seq(z, y, 1 - c)
    theirs = pl.ds(pl.multiple_of((1 - c) * 576, 16), 576)

    def to_mate(k, src, dst):
        return pltpu.make_async_remote_copy(
            src_ref=src, dst_ref=dst, send_sem=psem_s.at[k], recv_sem=psem_r.at[k],
            device_id=(x, mate), device_id_type=MESH,
        )

    att_copy = to_mate(0, attT.at[theirs], paT)
    cot_copies = [to_mate(1 + p, cp.at[:, COLS[p]], pc.at[:, COLS[p]]) for p in range(NP)]
    att_copy.start()

    def block(j, cols):
        own = attT[pl.ds(pl.multiple_of(c * 576 + j * 144, 16), 144), :]
        other = paT[pl.ds(pl.multiple_of(j * 144, 16), 144), :]
        return dot(own, cp[:, cols]) + dot(other, pc[:, cols])

    def x_copy(k, src, dst, s, r):
        return pltpu.make_async_remote_copy(
            src_ref=src, dst_ref=dst.at[k], send_sem=s.at[k], recv_sem=r.at[k],
            device_id=((x + k + 1) % XS, me), device_id_type=MESH,
        )

    def y_copy(k, src, dst, s, r):
        return pltpu.make_async_remote_copy(
            src_ref=src, dst_ref=dst.at[k], send_sem=s.at[k], recv_sem=r.at[k],
            device_id=(x, seq(z, (y + k + 1) % YS, c)), device_id_type=MESH,
        )

    def first(k, p):
        return x_copy(k, gsp[p].at[k], grp[p], gsem_s.at[p], gsem_r.at[p])

    def second(k, p):
        return y_copy(k, hsp[p].at[(y + k + 1) % YS], hrp[p], hsem_s.at[p], hsem_r.at[p])

    def cot_part(p):
        arrived(3 + p, csp[p], crp[p])
        cp[:, COLS[p]] = dot(to_patch, crp[p][...].reshape(256, WIDTHS[p])).astype(BF16)
        cot_copies[p].start()

    def blocks(p):
        cot_copies[p].wait()
        for k in range(3):
            gsp[p][k] = block((x + k + 1 + p) % XS, COLS[p]).astype(BF16)
            first(k, p).start()
        gop[p][...] = block((x + p) % XS, COLS[p])

    cot_part(0)
    att_f = dot(to_frame, attT[...], NT).astype(BF16)
    att_copy.wait()
    blocks(0)
    ms[...] = dot(att_f, outw[...]).astype(BF16).reshape(SEQ, 4, INNER)
    keep(1, ms, mixed_o).start()
    cot_part(1)
    batch(1, ms, mixed_o, 0, 2 * BATCH)
    blocks(1)
    cot_part(2)
    batch(1, ms, mixed_o, 2)

    @pl.loop(0, 2)
    def _(n):
        out = dot(outw[pl.ds(pl.multiple_of(n * 576, 16), 576), :], cp[...], NT)
        for i in range(8):
            gaT[n * 8 + i] = out[HD * i : HD * i + HD].astype(BF16)

    blocks(2)
    batch(1, ms, mixed_o, 3)

    def first_sum(p):
        total = gop[p][...]
        for k in range(3):
            first(k, p).wait()
            total = total + grp[p][k].astype(F32)
        for d in range(4):
            hsp[p][d] = total[36 * d : 36 * d + 36].astype(BF16)
        for k in range(3):
            second(k, p).start()

    roots = [seq(4 * c + (x + p) % XS, y, c) for p in range(NP)]
    def z_copy(p):
        return pltpu.make_async_remote_copy(
            src_ref=zsp[p], dst_ref=zrp[p].at[z], send_sem=zsem_s.at[p], recv_sem=zsem_r.at[p],
            device_id=(x, roots[p]), device_id_type=MESH,
        )

    def second_sum(p):
        total = hsp[p][y].astype(F32)
        for k in range(3):
            second(k, p).wait()
            total = total + hrp[p][k].astype(F32)
        zsp[p][...] = total.astype(BF16)

        @pl.when(roots[p] != me)
        def _():
            z_copy(p).start()

        @pl.when(roots[p] == me)
        def _():
            zrp[p][z] = zsp[p][...]

    def b_copy(k, p):
        dx, dc = OTHERS[k]
        return pltpu.make_async_remote_copy(
            src_ref=ogsp[p].at[(c + dc) % CS], dst_ref=ogrp[p], send_sem=bsem_s.at[p, k], recv_sem=bsem_r.at[p],
            device_id=((x + dx) % XS, seq(z, y, (c + dc) % CS)), device_id_type=MESH,
        )

    def z_sum(p):
        @pl.when(roots[p] == me)
        def _():
            part = zrp[p].at[pl.ds(0, ZS - 1)]
            pltpu.make_async_copy(part, part, zsem_r.at[p]).wait()
            total = zrp[p][0].astype(F32)
            for k in range(1, ZS):
                total = total + zrp[p][k].astype(F32)
            ogsp[p][0] = total[:18].astype(BF16)
            ogsp[p][1] = total[18:].astype(BF16)
            for k in range(len(OTHERS)):
                b_copy(k, p).start()

    def last(p):
        @pl.when(roots[p] == me)
        def _():
            og_o[:, COLS[p]] = ogsp[p][c].astype(F32)
            for k in range(len(OTHERS)):
                b_copy(k, p).wait_send()

        @pl.when(roots[p] != me)
        def _():
            z_copy(p).wait_send()
            b_copy(0, p).wait_recv()
            og_o[:, COLS[p]] = ogrp[p][...].astype(F32)

    def backward(n):
        outs = ([], [], [])
        for t in range(GROUP):
            h = n * GROUP + t
            ws, ds = [], []
            for i in range(2):
                w = w32s[i, h]
                dw = dot(qkvT[2 * HEADS + h, :, lanes(i)], gaT[h, :, lanes(i)], TN)
                ds.append((w * (dw - jnp.sum(w * dw, axis=0, keepdims=True)) * SCALE).astype(BF16))
                ws.append(w.astype(BF16))
            ds = diagonal(ds)
            outs[0].append(dot(qkvT[HEADS + h], ds))
            outs[1].append(dot(qkvT[h], ds, NT))
            outs[2].append(dot(gaT[h], diagonal(ws), NT))
        for u in range(3):
            gpT[group_rows(n, INNER * u), :] = jnp.concatenate(outs[u], axis=0).astype(BF16)
    @pl.loop(0, 2)
    def _(n):
        backward(n)
        batch(1, ms, mixed_o, n + 4)

    first_sum(0)
    @pl.loop(2, 4)
    def _(n):
        backward(n)
        pl.when(n == 2)(lambda: batch(1, ms, mixed_o, 6))

    first_sum(1)

    glatT[...] = dot(inw[...], gpT[...]).astype(BF16)

    gs[...] = dot(to_frame, glatT[...], NT).astype(BF16).reshape(SEQ, 4, INNER)
    first_sum(2)

    keep(2, gs, glat_o).start()
    batch(2, gs, glat_o, 0, 9)
    second_sum(0)
    second_sum(1)
    batch(2, gs, glat_o, 9 // BATCH, 9)
    second_sum(2)
    batch(2, gs, glat_o, (9 + 9) // BATCH, SEQ - 1 - 9 - 9)
    for p in range(NP):
        z_sum(p)
    for p in range(NP):
        last(p)
    og_copy = pltpu.make_async_copy(og_o, og_hbm, wsem.at[5])
    og_copy.start()
    sent(0, xs)
    for p in range(NP):
        sent(3 + p, csp[p])
    sent(1, ms)
    sent(2, gs)
    arrived(1, ms, mixed_o)
    arrived(2, gs, glat_o)
    og_copy.wait()


def unpack(mixed, glat, og, mixed_o, glat_o, og_o):
    mixed_o[0, 0] = mixed[...].reshape(256, INNER)
    glat_o[0, 0] = glat[...].reshape(256, INNER)
    og_o[...] = og[...]


def body(latents, in_weight, out_weight, cotangent, clip_lengths):
    width = latents.shape[3]
    vmem = pl.BlockSpec(memory_space=pltpu.VMEM)
    hbm = pl.BlockSpec(memory_space=pl.ANY)
    msg = (SEQ, 4, INNER)
    tok = (256, INNER)
    dma = pltpu.SemaphoreType.DMA
    mixed, grad_latents, out_grad = pl.pallas_call(
        kernel,
        out_shape=[
            jax.ShapeDtypeStruct(msg, BF16),
            jax.ShapeDtypeStruct(msg, BF16),
            jax.ShapeDtypeStruct((18, INNER), F32),
        ],
        in_specs=[hbm] * 5,
        out_specs=[hbm] * 3,
        scratch_shapes=[pltpu.VMEM(tok, BF16)] * 2
        + [pltpu.VMEM(msg, BF16)] * 4
        + [
            pltpu.VMEM((INNER, 3 * INNER), BF16),
            pltpu.VMEM((3 * INNER, INNER), BF16),
            pltpu.VMEM((INNER, INNER), BF16),
            pltpu.VMEM((3 * HEADS, HD, 256), BF16),
            pltpu.VMEM((2, HEADS, 128, 128), F32),
            pltpu.VMEM((INNER, 256), BF16),
            pltpu.VMEM(tok, BF16),
            pltpu.VMEM((HEADS, HD, 256), BF16),
            pltpu.VMEM((3 * INNER, 256), BF16),
            pltpu.VMEM((INNER, 256), BF16),
            pltpu.VMEM((576, 256), BF16),
            pltpu.VMEM(tok, BF16),
            pltpu.VMEM((128, 128), F32),
            pltpu.VMEM((18, INNER), F32),
            pltpu.SMEM((1, 4), jnp.int32),
            dma((6,)), dma((3 + NP,)), dma((3 + NP, 1)), dma((3 + NP,)), dma((1 + NP,)), dma((1 + NP,)),
            dma((NP, 3)), dma((NP, 3)), dma((NP, 3)), dma((NP, 3)), dma((NP,)), dma((NP,)),
            dma((NP, 7)), dma((NP,)),
        ]
        + [pltpu.VMEM((SEQ, 4, w), BF16) for w in WIDTHS] * 2
        + [pltpu.VMEM((3, 144, w), BF16) for w in WIDTHS] * 2
        + [pltpu.VMEM((144, w), F32) for w in WIDTHS]
        + [pltpu.VMEM((4, 36, w), BF16) for w in WIDTHS]
        + [pltpu.VMEM((3, 36, w), BF16) for w in WIDTHS]
        + [pltpu.VMEM((36, w), BF16) for w in WIDTHS]
        + [pltpu.VMEM((ZS, 36, w), BF16) for w in WIDTHS]
        + [pltpu.VMEM((2, 18, w), BF16) for w in WIDTHS]
        + [pltpu.VMEM((18, w), BF16) for w in WIDTHS],
        compiler_params=pltpu.CompilerParams(
            collective_id=0, has_side_effects=True, vmem_limit_bytes=52 << 20
        ),
        name="sublayer",
    )(
        latents.reshape(256, width), cotangent.reshape(256, width), clip_lengths, in_weight, out_weight,
    )
    return pl.pallas_call(
        unpack,
        out_shape=[
            jax.ShapeDtypeStruct(latents.shape, BF16),
            jax.ShapeDtypeStruct(latents.shape, BF16),
            jax.ShapeDtypeStruct((18, INNER), F32),
        ],
        in_specs=[vmem] * 3,
        out_specs=[vmem] * 3,
        compiler_params=pltpu.CompilerParams(vmem_limit_bytes=8 << 20),
        name="unpack",
    )(mixed, grad_latents, out_grad)


def solution(mesh):
    placed = (P("dp", "seq", None, None), P(), P(), P("dp", "seq", None, None), P("dp", None))
    return jax.shard_map(
        body,
        mesh=mesh,
        in_specs=placed,
        out_specs=(P("dp", "seq", None, None), P("dp", "seq", None, None), P("seq", None)),
        check_vma=False,
    )
```
